32 devices in a mesh: scen: 4 (over y, x), slab: 8 (over z, core).
Axes of the slice: x: 2, y: 2, z: 4, core: 2. Of those that a mesh axis runs over, the one named last changes fastest.
Arguments:
- start: float32 [4, 64, 256, 256], P('scen', 'slab'), may hold values from 0 to 2
- flow_east: float32 [4, 64, 256, 256], P('scen', 'slab'), may hold values from 0.3 to 1.2
- flow_north: float32 [4, 64, 256, 256], P('scen', 'slab'), may hold values from 0.3 to 1.2
- wells: int32 [64, 256, 256], P('slab'), may hold values 0 or 1
- monitors: int32 [64, 256, 256], P('slab'), may hold values 0 or 1
- control: float32 [4, 16, 4096], P('scen', 'slab'), may hold values from -3 to 3
- multiplier: float32 [4, 16, 4096], P('scen', 'slab'), may hold values from -3 to 3
- threshold: float32 [1], replicated, may hold values from 0.8 to 1.3
Outputs:
- final_fields: float32 [4, 64, 256, 256], P('scen', 'slab')
- consensus_next: float32 [16, 4096], P('slab')
- multiplier_next: float32 [4, 16, 4096], P('scen', 'slab')
- cvar: float32 [1], replicated
The draws below stay inside these ranges and needn't reach their ends.
All inputs are finite; a program needn't handle non-finite values. No bound on the sum of `wells` or of `monitors` on one device may be relied on, other than what follows from the above.
Results may differ from the reference program's by a relative error of at most 0.00002.
Values sent between devices are 32-bit elements; how exact they have to be, the bound alone decides.
A program may use at most 192 MiB of HBM per device.

```python
import jax
import jax.numpy as jnp
from jax import lax

NX = 256
NY = 256
STEPS = 4
SCEN = 4
NZ = 64
NZC = 16
CC = 4096


def plant(drawn, stream_key, smallest, largest):
    longest = drawn.shape.index(max(drawn.shape))
    spots = []
    for shift in (0, 1):
        where = [jax.random.randint(jax.random.fold_in(stream_key, axis), (), 0, length) for axis, length in enumerate(drawn.shape)]
        where[longest] = (where[longest] + shift) % drawn.shape[longest]
        spots.append(tuple(where))
    return drawn.at[spots[0]].set(smallest).at[spots[1]].set(largest)


def block_scale(rng, shape, split, least, high):
    def one(position, blocks):
        heights = jax.random.uniform(jax.random.fold_in(jax.random.fold_in(rng, 6), position), (blocks,), jnp.float32, least / len(split), high / len(split))
        return jnp.repeat(jnp.exp(heights), shape[position] // blocks).reshape((-1,) + (1,) * (len(shape) - position - 1))

    factor_of = one(*split[0])
    for cut in split[1:]:
        factor_of = factor_of * one(*cut)
    return factor_of


def noise(own_key, dims, width, bound, split=(), held_as=jnp.bfloat16):
    entries = jax.random.normal(own_key, dims, jnp.float32) * width
    if len(split) > 0:
        entries = block_scale(own_key, dims, split, -0.22, 0.18) * entries
    return jnp.clip(entries, min=-bound, max=bound).astype(held_as)


def setup_inputs(seed: int = 0) -> dict:
    keys = jax.random.split(jax.random.key(seed), 9)
    return {
        "start": jnp.clip(2.0 * jax.random.uniform(keys[0], (SCEN, NZ, NX, NY), jnp.float32) ** block_scale(keys[0], (SCEN, NZ, NX, NY), ((0, 4), (1, 8)), -0.2, 0.2), 0.0, 2.0),
        "flow_east": jnp.clip(0.3 + 0.90000004 * jax.random.uniform(keys[1], (SCEN, NZ, NX, NY), jnp.float32) ** block_scale(keys[1], (SCEN, NZ, NX, NY), ((0, 4), (1, 8)), -0.2, 0.2), 0.3, 1.2),
        "flow_north": jnp.clip(0.3 + 0.90000004 * jax.random.uniform(keys[2], (SCEN, NZ, NX, NY), jnp.float32) ** block_scale(keys[2], (SCEN, NZ, NX, NY), ((0, 4), (1, 8)), -0.2, 0.2), 0.3, 1.2),
        "wells": plant((jax.random.randint(keys[3], (NZ, NX, NY), 0, 4) < 1).astype(jnp.int32), jax.random.fold_in(keys[3], 1), 0, 1),
        "monitors": plant((jax.random.randint(keys[4], (NZ, NX, NY), 0, 4) < 1).astype(jnp.int32), jax.random.fold_in(keys[4], 1), 0, 1),
        "control": noise(keys[5], (SCEN, NZC, CC), 0.5, 3.0, ((0, 4), (1, 8)), jnp.float32),
        "multiplier": noise(keys[6], (SCEN, NZC, CC), 0.5, 3.0, ((0, 4), (1, 8)), jnp.float32),
        "threshold": jnp.clip(jax.random.uniform(keys[7], (1,), jnp.float32, 0.8, 1.3), 0.8, 1.3),
    }


EPS_LIMIT = 0.01
TIME_STEP = 0.25
DIFF_FLAT = 0.1
DIFF_VERTICAL = 0.25
BETA_LEVEL = 0.75
SOFT_WIDTH = 0.25

def pad_axis(field, which_axis, low_pad, high_pad):
    widths = [(0, 0)] * field.ndim
    widths[which_axis] = (low_pad, high_pad)
    return jnp.pad(field, widths)

def second_difference(padded, field, which_axis):
    length = field.shape[which_axis]
    upper_cells = lax.slice_in_dim(padded, 2, length + 2, axis=which_axis)
    lower_cells = lax.slice_in_dim(padded, 0, length, axis=which_axis)
    return upper_cells - 2.0 * field + lower_cells

def divergence(field, velocity, which_axis):
    length = field.shape[which_axis]
    padded = pad_axis(field, which_axis, 1, 1)
    lower_cells = lax.slice_in_dim(padded, 0, length, axis=which_axis)
    upper_cells = lax.slice_in_dim(padded, 2, length + 2, axis=which_axis)
    backward = field - lower_cells
    forward = upper_cells - field
    product = backward * forward
    weight = (product + jnp.sqrt(product * product + EPS_LIMIT * EPS_LIMIT)) / (backward * backward + forward * forward + EPS_LIMIT)
    face_value = field + 0.5 * weight * (backward / 3.0 + 2.0 * forward / 3.0)
    fluxes = velocity * face_value
    previous = lax.slice_in_dim(pad_axis(fluxes, which_axis, 1, 0), 0, length, axis=which_axis)
    return fluxes - previous

def horizontal(field, flow_east, flow_north, rate):
    advect = divergence(field, flow_east, 1) + divergence(field, flow_north, 2)
    spread = second_difference(pad_axis(field, 1, 1, 1), field, 1) + second_difference(pad_axis(field, 2, 1, 1), field, 2)
    return -advect + DIFF_FLAT * spread - rate * field

def prolong(coarse, row_count, column_count):
    plane_count = coarse.shape[0]
    cube = coarse.reshape(plane_count, 1, row_count // 4, 1, column_count // 4, 1)
    cube = jnp.broadcast_to(cube, (plane_count, 4, row_count // 4, 4, column_count // 4, 4))
    return cube.reshape(plane_count * 4, row_count, column_count)

def restrict(fine):
    plane_count, row_count, column_count = fine.shape
    blocks = fine.reshape(plane_count // 4, 4, row_count // 4, 4, column_count // 4, 4).sum(axis=(1, 3, 5))
    return blocks.reshape(plane_count // 4, row_count // 4 * (column_count // 4))

def forward_run(start, flow_east, flow_north, rate):
    field = start
    for step_index in range(STEPS):
        vertical = second_difference(pad_axis(field, 0, 1, 1), field, 0)
        field = field + TIME_STEP * (horizontal(field, flow_east, flow_north, rate) + DIFF_VERTICAL * vertical)
    return field

def reference(start, flow_east, flow_north, wells, monitors, control, multiplier, threshold):
    consensus = lax.optimization_barrier(jnp.sum(control + multiplier, axis=0)) / SCEN
    wells_float = wells.astype(jnp.float32)
    monitor_float = monitors.astype(jnp.float32)
    rate = wells_float * prolong(consensus, NX, NY)
    count = jnp.maximum(jnp.sum(monitor_float), 1.0)
    coarse_cells = NZ * NX * NY / 64.0

    def one_scenario(inputs):
        first, east, north = inputs
        final_field, pullback = jax.vjp(lambda rate_field: forward_run(first, east, north, rate_field), rate)
        loss = jnp.sum(monitor_float * final_field * final_field) / count
        scaled = (loss - threshold[0]) / SOFT_WIDTH
        weight = jax.nn.sigmoid(scaled) / ((1.0 - BETA_LEVEL) * SCEN)
        soft_term = SOFT_WIDTH * jax.nn.softplus(scaled) / ((1.0 - BETA_LEVEL) * SCEN)
        adjoint_start = weight * 2.0 * monitor_float * final_field / count
        rate_grad, = pullback(adjoint_start)
        gradient = coarse_cells * restrict(wells_float * rate_grad)
        return (final_field, soft_term, gradient)
    final_fields, soft_terms, gradients = lax.map(one_scenario, (start, flow_east, flow_north))
    consensus_next = consensus - lax.optimization_barrier(jnp.sum(gradients, axis=0))
    multiplier_next = multiplier + control - consensus_next[None]
    cvar = threshold + jnp.sum(soft_terms)
    return (final_fields, consensus_next, multiplier_next, cvar)
```

```python
import functools

import jax
import jax.numpy as jnp
from jax import lax
from jax.experimental import pallas as pl
from jax.experimental.pallas import tpu as pltpu
from jax.sharding import PartitionSpec as P

STEPS = 4
EPS_LIMIT = 0.01
TIME_STEP = 0.25
DIFF_FLAT = 0.1
DIFF_VERTICAL = 0.25
BETA_LEVEL = 0.75
SOFT_WIDTH = 0.25

LANES = 128
CELL = 4
CHUNKS = 4

DT_FLAT = TIME_STEP * DIFF_FLAT
DT_VERT = TIME_STEP * DIFF_VERTICAL
KEEP = 1.0 - 2.0 * DT_VERT
MESH = pl.DeviceIdType.MESH
HIGHEST = lax.Precision.HIGHEST


def limiter(a, b, q):
    p = a * b
    s2 = p * p + EPS_LIMIT * EPS_LIMIT
    rs = lax.rsqrt(s2)
    rq = pl.reciprocal(q, approx=True)
    return (p + s2 * rs) * rq, rs, rq


def slopes(a, b, t, rs, rq, uw):
    rq2 = rq + rq
    uwt = uw * t
    da = uw + uwt * (b * rs - a * rq2)
    db = (uw + uw - DT_FLAT) + uwt * (a * rs - b * rq2)
    return da, db


def kernel(
    scen_count,
    slab_count,
    start_hbm,
    east_hbm,
    north_hbm,
    wells_hbm,
    monitors_hbm,
    control,
    multiplier,
    threshold,
    fields_hbm,
    consensus_next,
    multiplier_next,
    cvar,
    state,
    lam,
    grad,
    ux,
    uy,
    wells,
    monitors,
    decay,
    coef,
    halo,
    spread_in,
    spread,
    gathered,
    cons,
    shares,
    sums,
    pulls,
    totals,
    load_sem,
    out_sem,
    halo_send,
    halo_recv,
    cons_send,
    cons_recv,
    sum_send,
    sum_recv,
    pull_send,
    pull_recv,
):
    planes, rows, cols = start_hbm.shape[1:]
    pieces = cols // LANES
    size = rows // CHUNKS
    per_lane = LANES // (cols // CELL)
    group = CELL * per_lane
    groups = size // group
    tiles = rows // group
    coarse_planes = planes // CELL
    scen = lax.axis_index("scen")
    slab = lax.axis_index("slab")
    last = slab_count - 1
    lane = lax.broadcasted_iota(jnp.int32, (planes, LANES), 1)
    level = lax.broadcasted_iota(jnp.int32, (planes, LANES), 0)
    lane_first = lane == 0
    lane_last = lane == LANES - 1
    level_first = level == 0
    level_last = level == planes - 1
    zero = jnp.zeros((planes, LANES), jnp.float32)

    def get(ref, *where):
        return [ref[(*where, slice(None), pl.ds(i * LANES, LANES))] for i in range(pieces)]

    def put(ref, values, *where):
        for i in range(pieces):
            ref[(*where, slice(None), pl.ds(i * LANES, LANES))] = values[i]

    def ahead(vs):
        nexts = vs[1:] + [zero]
        return [pltpu.roll(jnp.where(lane_first, n, v), LANES - 1, 1) for v, n in zip(vs, nexts)]

    def behind(vs, fill):
        out = [jnp.where(lane_first, fill, pltpu.roll(vs[0], 1, 1))]
        for v, n in zip(vs[1:], vs[:-1]):
            out.append(pltpu.roll(jnp.where(lane_last, n, v), 1, 1))
        return out

    def vertical(vs, hs):
        out = []
        for v, h in zip(vs, hs):
            below = jnp.where(level_first, h, pltpu.roll(v, 1, 0))
            above = jnp.where(level_last, h, pltpu.roll(v, planes - 1, 0))
            out.append(below + above)
        return out

    arrays = (
        (start_hbm.at[0], state.at[0]),
        (east_hbm.at[0], ux),
        (north_hbm.at[0], uy),
        (wells_hbm, wells),
        (monitors_hbm, monitors),
    )

    def load(which, chunk):
        source, target = arrays[which]
        span = pl.ds(chunk * size, size)
        for z in range(planes):
            pltpu.make_async_copy(
                source.at[z, span, :], target.at[span, z, :], load_sem.at[which, chunk]
            ).start()

    def loaded(which, chunk):
        target = arrays[which][1].at[pl.ds(chunk * size, size)]
        pltpu.make_async_copy(target, target, load_sem.at[which, chunk]).wait()

    def load_chunk(chunk, carry):
        for which in range(4):
            load(which, chunk)
        return carry

    lax.fori_loop(0, CHUNKS, load_chunk, 0)

    def load_monitors(chunk, carry):
        load(4, chunk)
        return carry

    lax.fori_loop(0, CHUNKS, load_monitors, 0)

    gathered[scen] = control[0] + multiplier[0]

    def clear(x, carry):
        for i in range(2):
            put(halo, [zero] * pieces, i, x)
        return carry

    lax.fori_loop(0, rows, clear, 0)
    for k in range(STEPS + 1):
        put(state, [zero] * pieces, k, rows)
    for i in range(2):
        put(lam, [zero] * pieces, i, rows)
        put(lam, [zero] * pieces, i, rows + 1)
    for k in range(STEPS - 1):
        put(coef, [zero] * pieces, k, 0, rows)

    barrier = pltpu.get_barrier_semaphore()
    for d in range(1, slab_count):
        pl.semaphore_signal(
            barrier, inc=1, device_id={"slab": lax.rem(slab + d, slab_count)}, device_id_type=MESH
        )
    for d in range(1, scen_count):
        pl.semaphore_signal(
            barrier, inc=1, device_id={"scen": lax.rem(scen + d, scen_count)}, device_id_type=MESH
        )

    pl.semaphore_wait(barrier, slab_count + scen_count - 2)

    def everyone(axis, me, count, buffer, send_sem, recv_sem):
        copies = []
        for d in range(1, count):
            copies.append(
                pltpu.make_async_remote_copy(
                    src_ref=buffer.at[me],
                    dst_ref=buffer.at[me],
                    send_sem=send_sem.at[d - 1],
                    recv_sem=recv_sem.at[d - 1],
                    device_id={axis: lax.rem(me + d, count)},
                    device_id_type=MESH,
                )
            )
        return copies

    cons_copies = everyone("scen", scen, scen_count, gathered, cons_send, cons_recv)
    for copy in cons_copies:
        copy.start()

    def rise(source, e, chunk):
        return pltpu.make_async_remote_copy(
            src_ref=source,
            dst_ref=halo.at[e % 2, pl.ds(chunk * size, size), 0, :],
            send_sem=halo_send.at[e, 0, chunk],
            recv_sem=halo_recv.at[e, 0, chunk],
            device_id={"slab": jnp.minimum(slab + 1, last)},
            device_id_type=MESH,
        )

    def sink(source, e, chunk):
        return pltpu.make_async_remote_copy(
            src_ref=source,
            dst_ref=halo.at[e % 2, pl.ds(chunk * size, size), planes - 1, :],
            send_sem=halo_send.at[e, 1, chunk],
            recv_sem=halo_recv.at[e, 1, chunk],
            device_id={"slab": jnp.maximum(slab - 1, 0)},
            device_id_type=MESH,
        )

    def plane(ref, chunk, z):
        return ref.at[pl.ds(chunk * size, size), z, :]

    def send(ref, e, chunk):
        @pl.when(slab < last)
        def _():
            rise(plane(ref, chunk, planes - 1), e, chunk).start()

        @pl.when(slab > 0)
        def _():
            sink(plane(ref, chunk, 0), e, chunk).start()

    def arrived(e, chunk):
        here = halo.at[e % 2]

        @pl.when(slab > 0)
        def _():
            rise(plane(here, chunk, 0), e, chunk).wait_recv()

        @pl.when(slab < last)
        def _():
            sink(plane(here, chunk, planes - 1), e, chunk).wait_recv()

    def sent(ref, e, chunk):
        @pl.when(slab < last)
        def _():
            rise(plane(ref, chunk, planes - 1), e, chunk).wait_send()

        @pl.when(slab > 0)
        def _():
            sink(plane(ref, chunk, 0), e, chunk).wait_send()

    def first_send(chunk, carry):
        span = pl.ds(chunk * size, size)

        @pl.when(slab < last)
        def _():
            rise(start_hbm.at[0, planes - 1, span, :], 0, chunk).start()

        @pl.when(slab > 0)
        def _():
            sink(start_hbm.at[0, 0, span, :], 0, chunk).start()

        return carry

    lax.fori_loop(0, CHUNKS, first_send, 0)

    for copy in cons_copies:
        copy.wait()
    total = gathered[0]
    for s in range(1, scen_count):
        total = total + gathered[s]
    cons[...] = total / scen_count
    for k in range(tiles):
        part = cons[:, pl.ds(k * LANES, LANES)]
        spread_in[pl.ds(k * planes, planes), :] = jnp.concatenate(
            [jnp.broadcast_to(part[p : p + 1], (CELL, LANES)) for p in range(coarse_planes)], axis=0
        )
    wide = per_lane * cols
    repeat = (
        lax.broadcasted_iota(jnp.int32, (LANES, wide), 0)
        == lax.broadcasted_iota(jnp.int32, (LANES, wide), 1) // CELL
    ).astype(jnp.float32)
    spread[...] = TIME_STEP * jnp.dot(
        spread_in[...], repeat, precision=HIGHEST, preferred_element_type=jnp.float32
    )

    def forward(k, first, final, carry):
        source = state.at[k]
        target = state.at[k + 1]

        def row(x, h, tile, c, a, a2, g_before, mass, count):
            c_next = get(source, x + 1)
            if first:
                vx = [v * (TIME_STEP / 6.0) for v in get(ux, x)]
                vy = [v * (TIME_STEP / 6.0) for v in get(uy, x)]
                put(ux, vx, x)
                put(uy, vy, x)
                well = get(wells, x)
                d = []
                for i in range(pieces):
                    rate = spread[pl.ds(tile * planes, planes), pl.ds(h * cols + i * LANES, LANES)]
                    d.append(KEEP - rate * well[i].astype(jnp.float32))
                put(decay, d, x)
            else:
                vx = get(ux, x)
                vy = get(uy, x)
                d = get(decay, x)
            z = vertical(c, get(halo, k % 2, x))
            c6 = [6.0 * v for v in c]
            b = [n - v for n, v in zip(c_next, c)]
            b2 = [v * v + 0.5 * EPS_LIMIT for v in b]
            flux = []
            out_a, out_b = [], []
            for i in range(pieces):
                w, rs, rq = limiter(a[i], b[i], a2[i] + b2[i])
                t = a[i] + (b[i] + b[i])
                if not first:
                    da, db = slopes(a[i], b[i], t, rs, rq, vx[i] * w)
                    out_a.append(da)
                    out_b.append(db)
                flux.append(vx[i] * (c6[i] + w * t) - DT_FLAT * b[i])
            if not first:
                put(coef, out_a, k - 1, 0, x)
                put(coef, out_b, k - 1, 1, x)
            c_ahead = ahead(c)
            e = [n - v for n, v in zip(c_ahead, c)]
            f = behind(e, c[0])
            side = []
            out_a, out_b = [], []
            for i in range(pieces):
                w, rs, rq = limiter(f[i], e[i], (f[i] * f[i] + e[i] * e[i]) + EPS_LIMIT)
                t = f[i] + (e[i] + e[i])
                if not first:
                    da, db = slopes(f[i], e[i], t, rs, rq, vy[i] * w)
                    out_a.append(da)
                    out_b.append(db)
                side.append(vy[i] * (c6[i] + w * t) - DT_FLAT * e[i])
            if not first:
                put(coef, out_a, k - 1, 2, x)
                put(coef, out_b, k - 1, 3, x)
            side_before = behind(side, -DT_FLAT * c[0])
            new = []
            for i in range(pieces):
                moved = (flux[i] - g_before[i]) + (side[i] - side_before[i])
                new.append((c[i] * d[i] + DT_VERT * z[i]) - moved)
            put(target, new, x)
            if final:
                watch = [m.astype(jnp.float32) for m in get(monitors, x)]
                seed = [m * v for m, v in zip(watch, new)]
                put(lam, seed, 0, x)
                mass = [m + s * v for m, s, v in zip(mass, seed, new)]
                count = [m + s for m, s in zip(count, watch)]
            return c_next, b, b2, flux, mass, count

        def chunk_step(chunk, carry):
            if first:
                ahead_chunk = jnp.minimum(chunk + 1, CHUNKS - 1)

                @pl.when(chunk + 1 < CHUNKS)
                def _():
                    loaded(0, ahead_chunk)

                for which in range(1, 4):
                    loaded(which, chunk)
            if final:
                loaded(4, chunk)
            arrived(k, chunk)

            def group_step(g, carry):
                tile = chunk * groups + g
                for r in range(group):
                    carry = row(tile * group + r, r // CELL, tile, *carry)
                return carry

            carry = lax.fori_loop(0, groups, group_step, carry)
            if final:
                send(lam.at[0], k + 1, chunk)
                span = pl.ds(chunk * size, size)
                for z in range(planes):
                    pltpu.make_async_copy(
                        target.at[span, z, :], fields_hbm.at[0, z, span, :], out_sem.at[chunk]
                    ).start()
            else:
                send(target, k + 1, chunk)
            return carry

        c = get(source, 0)
        a2 = [v * v + 0.5 * EPS_LIMIT for v in c]
        g = [-DT_FLAT * v for v in c]
        none = [zero] * pieces if final else []
        return lax.fori_loop(0, CHUNKS, chunk_step, (c, c, a2, g, none, none))

    loaded(0, 0)
    forward(0, True, False, None)

    def middle(k, carry):
        forward(k, False, False, None)
        return carry

    lax.fori_loop(1, STEPS - 1, middle, 0)
    *_, mass, count = forward(STEPS - 1, False, True, None)
    sums[slab, pl.ds(0, planes), :] = functools.reduce(jnp.add, mass)
    sums[slab, pl.ds(planes, planes), :] = functools.reduce(jnp.add, count)
    sum_copies = everyone("slab", slab, slab_count, sums, sum_send, sum_recv)
    for copy in sum_copies:
        copy.start()

    def backward(k, begin, final):
        e = 2 * STEPS - 1 - k
        slot = (STEPS - 1 - k) % 2
        source = lam.at[slot]
        target = lam.at[1 - slot]

        def row(x, c, n, mu, am, bm_before):
            n2 = get(source, x + 2)
            mu_next = [p - q for p, q in zip(n2, n)]
            am_next = [p * q for p, q in zip(get(coef, k - 1, 0, x + 1), mu_next)]
            bm = [p * q for p, q in zip(get(coef, k - 1, 1, x), mu)]
            side = [p - q for p, q in zip(ahead(c), c)]
            sa = [p * q for p, q in zip(get(coef, k - 1, 2, x), side)]
            sb = [p * q for p, q in zip(get(coef, k - 1, 3, x), side)]
            sa_next = ahead(sa)
            sb_before = behind(sb, -DT_FLAT * c[0])
            vx = get(ux, x)
            vy = get(uy, x)
            d = get(decay, x)
            z = vertical(c, get(halo, e % 2, x))
            past = get(state, k, x)
            kept = [p * q for p, q in zip(past, c)]
            if not begin:
                kept = [p + q for p, q in zip(kept, get(grad, x))]
            new = []
            for i in range(pieces):
                pull = 6.0 * (vx[i] * mu[i] + vy[i] * side[i])
                pull += (am[i] - am_next[i]) + (bm_before[i] - bm[i])
                pull += (sa[i] - sa_next[i]) + (sb_before[i] - sb[i])
                new.append((c[i] * d[i] + DT_VERT * z[i]) + pull)
            if not final:
                put(grad, kept, x)
                put(target, new, x)
            return kept, new, (n, n2, mu_next, am_next, bm)

        def chunk_step(chunk, carry):
            arrived(e, chunk)
            if not final and not begin:
                sent(target, e - 1, chunk)

            def group_step(g, carry):
                tile = chunk * groups + g
                part = None
                for r in range(group):
                    x = tile * group + r
                    kept, new, carry = row(x, *carry)
                    if final:
                        past = get(state, 0, x)
                        well = get(wells, x)
                        term = [
                            (p + q * s) * w.astype(jnp.float32)
                            for p, q, s, w in zip(kept, past, new, well)
                        ]
                        part = term if r % CELL == 0 else [p + q for p, q in zip(part, term)]
                        if r % CELL == CELL - 1:
                            for i in range(pieces):
                                at = (r // CELL) * cols + i * LANES
                                spread[pl.ds(tile * planes, planes), pl.ds(at, LANES)] = part[i]
                return carry

            carry = lax.fori_loop(0, groups, group_step, carry)
            if not final:
                send(target, e + 1, chunk)
            return carry

        c = get(source, 0)
        n = get(source, 1)
        mu = [p - q for p, q in zip(n, c)]
        am = [p * q for p, q in zip(get(coef, k - 1, 0, 0), mu)]
        bm = [-DT_FLAT * p for p in c]
        lax.fori_loop(0, CHUNKS, chunk_step, (c, n, mu, am, bm))

    for k in range(STEPS - 1, 0, -1):
        backward(k, k == STEPS - 1, k == 1)

    narrow = (
        lax.broadcasted_iota(jnp.int32, (wide, LANES), 0) // CELL
        == lax.broadcasted_iota(jnp.int32, (wide, LANES), 1)
    ).astype(jnp.float32)
    flat = jnp.dot(spread[...], narrow, precision=HIGHEST, preferred_element_type=jnp.float32)
    short = tiles * coarse_planes
    fold = (
        lax.broadcasted_iota(jnp.int32, (short, tiles * planes), 0)
        == lax.broadcasted_iota(jnp.int32, (short, tiles * planes), 1) // CELL
    ).astype(jnp.float32)
    shares[...] = jnp.dot(fold, flat, precision=HIGHEST, preferred_element_type=jnp.float32)

    for copy in sum_copies:
        copy.wait()
    both = sums[0]
    for s in range(1, slab_count):
        both = both + sums[s]
    mass = jnp.full((8, LANES), jnp.sum(both[:planes]), jnp.float32)
    count = jnp.full((8, LANES), jnp.sum(both[planes:]), jnp.float32)
    count = jnp.maximum(count, 1.0)
    scaled = (mass / count - threshold[0]) / SOFT_WIDTH
    level_scale = (1.0 - BETA_LEVEL) * scen_count
    decline = jnp.exp(-jnp.abs(scaled))
    weight = jnp.where(scaled >= 0.0, 1.0, decline) / (1.0 + decline) / level_scale
    soft = SOFT_WIDTH * (jnp.maximum(scaled, 0.0) + jnp.log1p(decline)) / level_scale
    coarse_cells = planes * slab_count * rows * cols / float(CELL**3)
    factor = (-TIME_STEP * 2.0 * coarse_cells) * weight / count
    pulls[scen, pl.ds(0, short), :] = shares[...] * factor[0:1]
    pulls[scen, pl.ds(short, 8), :] = soft
    pull_copies = everyone("scen", scen, scen_count, pulls, pull_send, pull_recv)
    for copy in pull_copies:
        copy.start()

    def drain(chunk, carry):
        for e in range(STEPS):
            sent(state.at[e], e, chunk)
        sent(lam.at[1], 2 * STEPS - 3, chunk)
        sent(lam.at[0], 2 * STEPS - 2, chunk)
        target = state.at[STEPS, pl.ds(chunk * size, size)]
        pltpu.make_async_copy(target, target, out_sem.at[chunk]).wait()
        return carry

    lax.fori_loop(0, CHUNKS, drain, 0)

    for copy in pull_copies:
        copy.wait()
    all_pulls = pulls[0]
    for s in range(1, scen_count):
        all_pulls = all_pulls + pulls[s]
    totals[...] = all_pulls
    cvar[0] = threshold[0] + jnp.max(all_pulls[short:])
    for k in range(tiles):
        span = pl.ds(k * LANES, LANES)
        value = cons[:, span] - totals[pl.ds(k * coarse_planes, coarse_planes), :]
        consensus_next[:, span] = value
        multiplier_next[0, :, span] = (multiplier[0, :, span] + control[0, :, span]) - value


def on_device(start, flow_east, flow_north, wells, monitors, control, multiplier, threshold):
    scen_count = lax.axis_size("scen")
    slab_count = lax.axis_size("slab")
    _, planes, rows, cols = start.shape
    _, coarse_planes, coarse = control.shape
    per_lane = LANES // (cols // CELL)
    tiles = rows // (CELL * per_lane)
    short = tiles * coarse_planes
    f32 = jnp.float32
    dma = pltpu.SemaphoreType.DMA
    vmem = pltpu.VMEM
    exchanges = 2 * STEPS - 1
    anywhere = pl.BlockSpec(memory_space=pl.ANY)
    near = pl.BlockSpec(memory_space=pltpu.VMEM)
    scalar = pl.BlockSpec(memory_space=pltpu.SMEM)
    return pl.pallas_call(
        functools.partial(kernel, scen_count, slab_count),
        out_shape=(
            jax.ShapeDtypeStruct(start.shape, f32),
            jax.ShapeDtypeStruct((coarse_planes, coarse), f32),
            jax.ShapeDtypeStruct(control.shape, f32),
            jax.ShapeDtypeStruct((1,), f32),
        ),
        in_specs=[anywhere] * 5 + [near, near, scalar],
        out_specs=(anywhere, near, near, scalar),
        scratch_shapes=[
            vmem((STEPS + 1, rows + 1, planes, cols), f32),
            vmem((2, rows + 2, planes, cols), f32),
            vmem((rows, planes, cols), f32),
            vmem((rows, planes, cols), f32),
            vmem((rows, planes, cols), f32),
            vmem((rows, planes, cols), jnp.int32),
            vmem((rows, planes, cols), jnp.int32),
            vmem((rows, planes, cols), f32),
            vmem((STEPS - 1, 4, rows + 1, planes, cols), f32),
            vmem((2, rows, planes, cols), f32),
            vmem((tiles * planes, LANES), f32),
            vmem((tiles * planes, per_lane * cols), f32),
            vmem((scen_count, coarse_planes, coarse), f32),
            vmem((coarse_planes, coarse), f32),
            vmem((short, LANES), f32),
            vmem((slab_count, 2 * planes, LANES), f32),
            vmem((scen_count, short + 8, LANES), f32),
            vmem((short + 8, LANES), f32),
            dma((5, CHUNKS)),
            dma((CHUNKS,)),
            dma((exchanges, 2, CHUNKS)),
            dma((exchanges, 2, CHUNKS)),
            dma((scen_count - 1,)),
            dma((scen_count - 1,)),
            dma((slab_count - 1,)),
            dma((slab_count - 1,)),
            dma((scen_count - 1,)),
            dma((scen_count - 1,)),
        ],
        compiler_params=pltpu.CompilerParams(
            collective_id=0, has_side_effects=True, vmem_limit_bytes=62 * 1024 * 1024
        ),
        name="window",
    )(start, flow_east, flow_north, wells, monitors, control, multiplier, threshold)


def solution(mesh):
    placed = (
        P("scen", "slab", None, None),
        P("scen", "slab", None, None),
        P("scen", "slab", None, None),
        P("slab", None, None),
        P("slab", None, None),
        P("scen", "slab", None),
        P("scen", "slab", None),
        P(),
    )
    return jax.shard_map(
        on_device,
        mesh=mesh,
        in_specs=placed,
        out_specs=(P("scen", "slab", None, None), P("slab", None), P("scen", "slab", None), P()),
        check_vma=False,
    )
```

```python
import functools

import jax
import jax.numpy as jnp
from jax import lax
from jax.experimental import pallas as pl
from jax.experimental.pallas import tpu as pltpu
from jax.sharding import PartitionSpec as P

STEPS = 4
EPS_LIMIT = 0.01
TIME_STEP = 0.25
DIFF_FLAT = 0.1
DIFF_VERTICAL = 0.25
BETA_LEVEL = 0.75
SOFT_WIDTH = 0.25

LANES = 128
CELL = 4
CHUNKS = 2

DT_FLAT = TIME_STEP * DIFF_FLAT
DT_VERT = TIME_STEP * DIFF_VERTICAL
KEEP = 1.0 - 2.0 * DT_VERT
MESH = pl.DeviceIdType.MESH
HIGHEST = lax.Precision.HIGHEST


def limiter(a, b, q):
    p = a * b
    s2 = p * p + EPS_LIMIT * EPS_LIMIT
    rs = lax.rsqrt(s2)
    rq = pl.reciprocal(q, approx=True)
    return (p + s2 * rs) * rq, rs, rq


def slopes(a, b, t, rs, rq, uw):
    rq2 = rq + rq
    uwt = uw * t
    da = uw + uwt * (b * rs - a * rq2)
    db = (uw + uw - DT_FLAT) + uwt * (a * rs - b * rq2)
    return da, db


def kernel(
    scen_count,
    slab_count,
    start_hbm,
    east_hbm,
    north_hbm,
    wells_hbm,
    monitors_hbm,
    control,
    multiplier,
    threshold,
    fields_hbm,
    consensus_next,
    multiplier_next,
    cvar,
    state,
    lam,
    grad,
    ux,
    uy,
    wells,
    monitors,
    decay,
    coef,
    halo,
    spread_in,
    spread,
    gathered,
    cons,
    shares,
    sums,
    pulls,
    totals,
    load_sem,
    out_sem,
    halo_send,
    halo_recv,
    cons_send,
    cons_recv,
    sum_send,
    sum_recv,
    pull_send,
    pull_recv,
):
    planes, rows, cols = start_hbm.shape[1:]
    pieces = cols // LANES
    size = rows // CHUNKS
    per_lane = LANES // (cols // CELL)
    group = CELL * per_lane
    groups = size // group
    tiles = rows // group
    coarse_planes = planes // CELL
    scen = lax.axis_index("scen")
    slab = lax.axis_index("slab")
    last = slab_count - 1
    lane = lax.broadcasted_iota(jnp.int32, (planes, LANES), 1)
    level = lax.broadcasted_iota(jnp.int32, (planes, LANES), 0)
    lane_first = lane == 0
    lane_last = lane == LANES - 1
    level_first = level == 0
    level_last = level == planes - 1
    zero = jnp.zeros((planes, LANES), jnp.float32)

    def get(ref, *where):
        return [ref[(*where, slice(None), pl.ds(i * LANES, LANES))] for i in range(pieces)]

    def put(ref, values, *where):
        for i in range(pieces):
            ref[(*where, slice(None), pl.ds(i * LANES, LANES))] = values[i]

    def ahead(vs):
        nexts = vs[1:] + [zero]
        return [pltpu.roll(jnp.where(lane_first, n, v), LANES - 1, 1) for v, n in zip(vs, nexts)]

    def behind(vs, fill):
        out = [jnp.where(lane_first, fill, pltpu.roll(vs[0], 1, 1))]
        for v, n in zip(vs[1:], vs[:-1]):
            out.append(pltpu.roll(jnp.where(lane_last, n, v), 1, 1))
        return out

    def vertical(vs, hs):
        out = []
        for v, h in zip(vs, hs):
            below = jnp.where(level_first, h, pltpu.roll(v, 1, 0))
            above = jnp.where(level_last, h, pltpu.roll(v, planes - 1, 0))
            out.append(below + above)
        return out

    arrays = (
        (start_hbm.at[0], state.at[0]),
        (east_hbm.at[0], ux),
        (north_hbm.at[0], uy),
        (wells_hbm, wells),
        (monitors_hbm, monitors),
    )

    def load(which, chunk):
        source, target = arrays[which]
        span = pl.ds(chunk * size, size)
        for z in range(planes):
            pltpu.make_async_copy(
                source.at[z, span, :], target.at[span, z, :], load_sem.at[which, chunk]
            ).start()

    def loaded(which, chunk):
        target = arrays[which][1].at[pl.ds(chunk * size, size)]
        pltpu.make_async_copy(target, target, load_sem.at[which, chunk]).wait()

    def load_chunk(chunk, carry):
        for which in range(4):
            load(which, chunk)
        return carry

    lax.fori_loop(0, CHUNKS, load_chunk, 0)

    def load_monitors(chunk, carry):
        load(4, chunk)
        return carry

    lax.fori_loop(0, CHUNKS, load_monitors, 0)

    gathered[scen] = control[0] + multiplier[0]

    def clear(x, carry):
        for i in range(2):
            put(halo, [zero] * pieces, i, x)
        return carry

    lax.fori_loop(0, rows, clear, 0)
    for k in range(STEPS + 1):
        put(state, [zero] * pieces, k, rows)
    for i in range(2):
        put(lam, [zero] * pieces, i, rows)
        put(lam, [zero] * pieces, i, rows + 1)
    for k in range(STEPS - 1):
        put(coef, [zero] * pieces, k, 0, rows)

    barrier = pltpu.get_barrier_semaphore()
    for d in range(1, slab_count):
        pl.semaphore_signal(
            barrier, inc=1, device_id={"slab": lax.rem(slab + d, slab_count)}, device_id_type=MESH
        )
    for d in range(1, scen_count):
        pl.semaphore_signal(
            barrier, inc=1, device_id={"scen": lax.rem(scen + d, scen_count)}, device_id_type=MESH
        )

    pl.semaphore_wait(barrier, slab_count + scen_count - 2)

    def everyone(axis, me, count, buffer, send_sem, recv_sem):
        copies = []
        for d in range(1, count):
            copies.append(
                pltpu.make_async_remote_copy(
                    src_ref=buffer.at[me],
                    dst_ref=buffer.at[me],
                    send_sem=send_sem.at[d - 1],
                    recv_sem=recv_sem.at[d - 1],
                    device_id={axis: lax.rem(me + d, count)},
                    device_id_type=MESH,
                )
            )
        return copies

    cons_copies = everyone("scen", scen, scen_count, gathered, cons_send, cons_recv)
    for copy in cons_copies:
        copy.start()

    def rise(source, e, chunk):
        return pltpu.make_async_remote_copy(
            src_ref=source,
            dst_ref=halo.at[e % 2, pl.ds(chunk * size, size), 0, :],
            send_sem=halo_send.at[e, 0, chunk],
            recv_sem=halo_recv.at[e, 0, chunk],
            device_id={"slab": jnp.minimum(slab + 1, last)},
            device_id_type=MESH,
        )

    def sink(source, e, chunk):
        return pltpu.make_async_remote_copy(
            src_ref=source,
            dst_ref=halo.at[e % 2, pl.ds(chunk * size, size), planes - 1, :],
            send_sem=halo_send.at[e, 1, chunk],
            recv_sem=halo_recv.at[e, 1, chunk],
            device_id={"slab": jnp.maximum(slab - 1, 0)},
            device_id_type=MESH,
        )

    def plane(ref, chunk, z):
        return ref.at[pl.ds(chunk * size, size), z, :]

    def send(ref, e, chunk):
        @pl.when(slab < last)
        def _():
            rise(plane(ref, chunk, planes - 1), e, chunk).start()

        @pl.when(slab > 0)
        def _():
            sink(plane(ref, chunk, 0), e, chunk).start()

    def arrived(e, chunk):
        here = halo.at[e % 2]

        @pl.when(slab > 0)
        def _():
            rise(plane(here, chunk, 0), e, chunk).wait_recv()

        @pl.when(slab < last)
        def _():
            sink(plane(here, chunk, planes - 1), e, chunk).wait_recv()

    def sent(ref, e, chunk):
        @pl.when(slab < last)
        def _():
            rise(plane(ref, chunk, planes - 1), e, chunk).wait_send()

        @pl.when(slab > 0)
        def _():
            sink(plane(ref, chunk, 0), e, chunk).wait_send()

    def first_send(chunk, carry):
        span = pl.ds(chunk * size, size)

        @pl.when(slab < last)
        def _():
            rise(start_hbm.at[0, planes - 1, span, :], 0, chunk).start()

        @pl.when(slab > 0)
        def _():
            sink(start_hbm.at[0, 0, span, :], 0, chunk).start()

        return carry

    lax.fori_loop(0, CHUNKS, first_send, 0)

    for copy in cons_copies:
        copy.wait()
    total = gathered[0]
    for s in range(1, scen_count):
        total = total + gathered[s]
    cons[...] = total / scen_count
    for k in range(tiles):
        part = cons[:, pl.ds(k * LANES, LANES)]
        spread_in[pl.ds(k * planes, planes), :] = jnp.concatenate(
            [jnp.broadcast_to(part[p : p + 1], (CELL, LANES)) for p in range(coarse_planes)], axis=0
        )
    wide = per_lane * cols
    repeat = (
        lax.broadcasted_iota(jnp.int32, (LANES, wide), 0)
        == lax.broadcasted_iota(jnp.int32, (LANES, wide), 1) // CELL
    ).astype(jnp.float32)
    spread[...] = TIME_STEP * jnp.dot(
        spread_in[...], repeat, precision=HIGHEST, preferred_element_type=jnp.float32
    )

    def forward(k, first, final, carry):
        source = state.at[k]
        target = state.at[k + 1]

        def row(x, h, tile, c, a, a2, g_before, mass, count):
            c_next = get(source, x + 1)
            if first:
                vx = [v * (TIME_STEP / 6.0) for v in get(ux, x)]
                vy = [v * (TIME_STEP / 6.0) for v in get(uy, x)]
                put(ux, vx, x)
                put(uy, vy, x)
                well = get(wells, x)
                d = []
                for i in range(pieces):
                    rate = spread[pl.ds(tile * planes, planes), pl.ds(h * cols + i * LANES, LANES)]
                    d.append(KEEP - rate * well[i].astype(jnp.float32))
                put(decay, d, x)
            else:
                vx = get(ux, x)
                vy = get(uy, x)
                d = get(decay, x)
            z = vertical(c, get(halo, k % 2, x))
            c6 = [6.0 * v for v in c]
            b = [n - v for n, v in zip(c_next, c)]
            b2 = [v * v + 0.5 * EPS_LIMIT for v in b]
            flux = []
            out_a, out_b = [], []
            for i in range(pieces):
                w, rs, rq = limiter(a[i], b[i], a2[i] + b2[i])
                t = a[i] + (b[i] + b[i])
                if not first:
                    da, db = slopes(a[i], b[i], t, rs, rq, vx[i] * w)
                    out_a.append(da)
                    out_b.append(db)
                flux.append(vx[i] * (c6[i] + w * t) - DT_FLAT * b[i])
            if not first:
                put(coef, out_a, k - 1, 0, x)
                put(coef, out_b, k - 1, 1, x)
            c_ahead = ahead(c)
            e = [n - v for n, v in zip(c_ahead, c)]
            f = [v - n for v, n in zip(c, behind(c, zero))]
            side = []
            out_a, out_b = [], []
            for i in range(pieces):
                w, rs, rq = limiter(f[i], e[i], (f[i] * f[i] + e[i] * e[i]) + EPS_LIMIT)
                t = f[i] + (e[i] + e[i])
                if not first:
                    da, db = slopes(f[i], e[i], t, rs, rq, vy[i] * w)
                    out_a.append(da)
                    out_b.append(db)
                side.append(vy[i] * (c6[i] + w * t) - DT_FLAT * e[i])
            if not first:
                put(coef, out_a, k - 1, 2, x)
                put(coef, out_b, k - 1, 3, x)
            side_before = behind(side, -DT_FLAT * c[0])
            new = []
            for i in range(pieces):
                moved = (flux[i] - g_before[i]) + (side[i] - side_before[i])
                new.append((c[i] * d[i] + DT_VERT * z[i]) - moved)
            put(target, new, x)
            if final:
                watch = [m.astype(jnp.float32) for m in get(monitors, x)]
                seed = [m * v for m, v in zip(watch, new)]
                put(lam, seed, 0, x)
                mass = [m + s * v for m, s, v in zip(mass, seed, new)]
                count = [m + s for m, s in zip(count, watch)]
            return c_next, b, b2, flux, mass, count

        def chunk_step(chunk, carry):
            if first:
                ahead_chunk = jnp.minimum(chunk + 1, CHUNKS - 1)

                @pl.when(chunk + 1 < CHUNKS)
                def _():
                    loaded(0, ahead_chunk)

                for which in range(1, 4):
                    loaded(which, chunk)
            if final:
                loaded(4, chunk)
            arrived(k, chunk)

            def group_step(g, carry):
                tile = chunk * groups + g
                for r in range(group):
                    carry = row(tile * group + r, r // CELL, tile, *carry)
                return carry

            carry = lax.fori_loop(0, groups, group_step, carry, unroll=2)
            if final:
                send(lam.at[0], k + 1, chunk)
                span = pl.ds(chunk * size, size)
                for z in range(planes):
                    pltpu.make_async_copy(
                        target.at[span, z, :], fields_hbm.at[0, z, span, :], out_sem.at[chunk]
                    ).start()
            else:
                send(target, k + 1, chunk)
            return carry

        c = get(source, 0)
        a2 = [v * v + 0.5 * EPS_LIMIT for v in c]
        g = [-DT_FLAT * v for v in c]
        none = [zero] * pieces if final else []
        return lax.fori_loop(0, CHUNKS, chunk_step, (c, c, a2, g, none, none))

    loaded(0, 0)
    forward(0, True, False, None)

    def middle(k, carry):
        forward(k, False, False, None)
        return carry

    lax.fori_loop(1, STEPS - 1, middle, 0)
    *_, mass, count = forward(STEPS - 1, False, True, None)
    sums[slab, pl.ds(0, planes), :] = functools.reduce(jnp.add, mass)
    sums[slab, pl.ds(planes, planes), :] = functools.reduce(jnp.add, count)
    sum_copies = everyone("slab", slab, slab_count, sums, sum_send, sum_recv)
    for copy in sum_copies:
        copy.start()

    def backward(k, begin, final):
        e = 2 * STEPS - 1 - k
        slot = (STEPS - 1 - k) % 2
        source = lam.at[slot]
        target = lam.at[1 - slot]

        def row(x, c, n, mu, am, bm_before):
            n2 = get(source, x + 2)
            mu_next = [p - q for p, q in zip(n2, n)]
            am_next = [p * q for p, q in zip(get(coef, k - 1, 0, x + 1), mu_next)]
            bm = [p * q for p, q in zip(get(coef, k - 1, 1, x), mu)]
            side = [p - q for p, q in zip(ahead(c), c)]
            sa = [p * q for p, q in zip(get(coef, k - 1, 2, x), side)]
            sb = [p * q for p, q in zip(get(coef, k - 1, 3, x), side)]
            sa_next = ahead(sa)
            sb_before = behind(sb, -DT_FLAT * c[0])
            vx = get(ux, x)
            vy = get(uy, x)
            d = get(decay, x)
            z = vertical(c, get(halo, e % 2, x))
            past = get(state, k, x)
            kept = [p * q for p, q in zip(past, c)]
            if not begin:
                kept = [p + q for p, q in zip(kept, get(grad, x))]
            new = []
            for i in range(pieces):
                pull = 6.0 * (vx[i] * mu[i] + vy[i] * side[i])
                pull += (am[i] - am_next[i]) + (bm_before[i] - bm[i])
                pull += (sa[i] - sa_next[i]) + (sb_before[i] - sb[i])
                new.append((c[i] * d[i] + DT_VERT * z[i]) + pull)
            if not final:
                put(grad, kept, x)
                put(target, new, x)
            return kept, new, (n, n2, mu_next, am_next, bm)

        def chunk_step(chunk, carry):
            arrived(e, chunk)
            if not final and not begin:
                sent(target, e - 1, chunk)

            def group_step(g, carry):
                tile = chunk * groups + g
                part = None
                for r in range(group):
                    x = tile * group + r
                    kept, new, carry = row(x, *carry)
                    if final:
                        past = get(state, 0, x)
                        well = get(wells, x)
                        term = [
                            (p + q * s) * w.astype(jnp.float32)
                            for p, q, s, w in zip(kept, past, new, well)
                        ]
                        part = term if r % CELL == 0 else [p + q for p, q in zip(part, term)]
                        if r % CELL == CELL - 1:
                            for i in range(pieces):
                                at = (r // CELL) * cols + i * LANES
                                spread[pl.ds(tile * planes, planes), pl.ds(at, LANES)] = part[i]
                return carry

            carry = lax.fori_loop(0, groups, group_step, carry, unroll=2)
            if not final:
                send(target, e + 1, chunk)
            return carry

        c = get(source, 0)
        n = get(source, 1)
        mu = [p - q for p, q in zip(n, c)]
        am = [p * q for p, q in zip(get(coef, k - 1, 0, 0), mu)]
        bm = [-DT_FLAT * p for p in c]
        lax.fori_loop(0, CHUNKS, chunk_step, (c, n, mu, am, bm))

    for k in range(STEPS - 1, 0, -1):
        backward(k, k == STEPS - 1, k == 1)

    narrow = (
        lax.broadcasted_iota(jnp.int32, (wide, LANES), 0) // CELL
        == lax.broadcasted_iota(jnp.int32, (wide, LANES), 1)
    ).astype(jnp.float32)
    flat = jnp.dot(spread[...], narrow, precision=HIGHEST, preferred_element_type=jnp.float32)
    short = tiles * coarse_planes
    fold = (
        lax.broadcasted_iota(jnp.int32, (short, tiles * planes), 0)
        == lax.broadcasted_iota(jnp.int32, (short, tiles * planes), 1) // CELL
    ).astype(jnp.float32)
    shares[...] = jnp.dot(fold, flat, precision=HIGHEST, preferred_element_type=jnp.float32)

    for copy in sum_copies:
        copy.wait()
    both = sums[0]
    for s in range(1, slab_count):
        both = both + sums[s]
    mass = jnp.full((8, LANES), jnp.sum(both[:planes]), jnp.float32)
    count = jnp.full((8, LANES), jnp.sum(both[planes:]), jnp.float32)
    count = jnp.maximum(count, 1.0)
    scaled = (mass / count - threshold[0]) / SOFT_WIDTH
    level_scale = (1.0 - BETA_LEVEL) * scen_count
    decline = jnp.exp(-jnp.abs(scaled))
    weight = jnp.where(scaled >= 0.0, 1.0, decline) / (1.0 + decline) / level_scale
    soft = SOFT_WIDTH * (jnp.maximum(scaled, 0.0) + jnp.log1p(decline)) / level_scale
    coarse_cells = planes * slab_count * rows * cols / float(CELL**3)
    factor = (-TIME_STEP * 2.0 * coarse_cells) * weight / count
    pulls[scen, pl.ds(0, short), :] = shares[...] * factor[0:1]
    pulls[scen, pl.ds(short, 8), :] = soft
    pull_copies = everyone("scen", scen, scen_count, pulls, pull_send, pull_recv)
    for copy in pull_copies:
        copy.start()

    def drain(chunk, carry):
        for e in range(STEPS):
            sent(state.at[e], e, chunk)
        sent(lam.at[1], 2 * STEPS - 3, chunk)
        sent(lam.at[0], 2 * STEPS - 2, chunk)
        target = state.at[STEPS, pl.ds(chunk * size, size)]
        pltpu.make_async_copy(target, target, out_sem.at[chunk]).wait()
        return carry

    lax.fori_loop(0, CHUNKS, drain, 0)

    for copy in pull_copies:
        copy.wait()
    all_pulls = pulls[0]
    for s in range(1, scen_count):
        all_pulls = all_pulls + pulls[s]
    totals[...] = all_pulls
    cvar[0] = threshold[0] + jnp.max(all_pulls[short:])
    for k in range(tiles):
        span = pl.ds(k * LANES, LANES)
        value = cons[:, span] - totals[pl.ds(k * coarse_planes, coarse_planes), :]
        consensus_next[:, span] = value
        multiplier_next[0, :, span] = (multiplier[0, :, span] + control[0, :, span]) - value


def on_device(start, flow_east, flow_north, wells, monitors, control, multiplier, threshold):
    scen_count = lax.axis_size("scen")
    slab_count = lax.axis_size("slab")
    _, planes, rows, cols = start.shape
    _, coarse_planes, coarse = control.shape
    per_lane = LANES // (cols // CELL)
    tiles = rows // (CELL * per_lane)
    short = tiles * coarse_planes
    f32 = jnp.float32
    dma = pltpu.SemaphoreType.DMA
    vmem = pltpu.VMEM
    exchanges = 2 * STEPS - 1
    anywhere = pl.BlockSpec(memory_space=pl.ANY)
    near = pl.BlockSpec(memory_space=pltpu.VMEM)
    scalar = pl.BlockSpec(memory_space=pltpu.SMEM)
    return pl.pallas_call(
        functools.partial(kernel, scen_count, slab_count),
        out_shape=(
            jax.ShapeDtypeStruct(start.shape, f32),
            jax.ShapeDtypeStruct((coarse_planes, coarse), f32),
            jax.ShapeDtypeStruct(control.shape, f32),
            jax.ShapeDtypeStruct((1,), f32),
        ),
        in_specs=[anywhere] * 5 + [near, near, scalar],
        out_specs=(anywhere, near, near, scalar),
        scratch_shapes=[
            vmem((STEPS + 1, rows + 1, planes, cols), f32),
            vmem((2, rows + 2, planes, cols), f32),
            vmem((rows, planes, cols), f32),
            vmem((rows, planes, cols), f32),
            vmem((rows, planes, cols), f32),
            vmem((rows, planes, cols), jnp.int32),
            vmem((rows, planes, cols), jnp.int32),
            vmem((rows, planes, cols), f32),
            vmem((STEPS - 1, 4, rows + 1, planes, cols), f32),
            vmem((2, rows, planes, cols), f32),
            vmem((tiles * planes, LANES), f32),
            vmem((tiles * planes, per_lane * cols), f32),
            vmem((scen_count, coarse_planes, coarse), f32),
            vmem((coarse_planes, coarse), f32),
            vmem((short, LANES), f32),
            vmem((slab_count, 2 * planes, LANES), f32),
            vmem((scen_count, short + 8, LANES), f32),
            vmem((short + 8, LANES), f32),
            dma((5, CHUNKS)),
            dma((CHUNKS,)),
            dma((exchanges, 2, CHUNKS)),
            dma((exchanges, 2, CHUNKS)),
            dma((scen_count - 1,)),
            dma((scen_count - 1,)),
            dma((slab_count - 1,)),
            dma((slab_count - 1,)),
            dma((scen_count - 1,)),
            dma((scen_count - 1,)),
        ],
        compiler_params=pltpu.CompilerParams(
            collective_id=0, has_side_effects=True, vmem_limit_bytes=62 * 1024 * 1024
        ),
        name="window",
    )(start, flow_east, flow_north, wells, monitors, control, multiplier, threshold)


def solution(mesh):
    placed = (
        P("scen", "slab", None, None),
        P("scen", "slab", None, None),
        P("scen", "slab", None, None),
        P("slab", None, None),
        P("slab", None, None),
        P("scen", "slab", None),
        P("scen", "slab", None),
        P(),
    )
    return jax.shard_map(
        on_device,
        mesh=mesh,
        in_specs=placed,
        out_specs=(P("scen", "slab", None, None), P("slab", None), P("scen", "slab", None), P()),
        check_vma=False,
    )
```
